32 devices in a mesh: section: 2 (over core), expert: 16 (over z, y, x).
Axes of the slice: x: 2, y: 2, z: 4, core: 2. Of those that a mesh axis runs over, the one named last changes fastest.
Arguments:
- hidden: bfloat16 [2, 2048, 2048], P('section', 'expert'), may hold values from -6 to 6
- out_grad: bfloat16 [2, 2048, 2048], P('section', 'expert'), may hold values from -6 to 6
- expert_ids: int32 [2, 2048, 8], P('section', 'expert'), may hold values from 0 to 15, all different within a row; in each aligned block of 128 rows (0 to 127, 128 to 255, ..., all dimensions but the last counted through in order) at most 80 rows name the same one
- gate_weight: bfloat16 [2, 2048, 8], P('section', 'expert'), may hold values from 0.029907227 to 0.5
- w_gate: bfloat16 [2, 16, 2048, 768], P('section', 'expert'), may hold values from -0.125 to 0.125
- w_up: bfloat16 [2, 16, 2048, 768], P('section', 'expert'), may hold values from -0.125 to 0.125
- w_down: bfloat16 [2, 16, 768, 2048], P('section', 'expert'), may hold values from -0.21875 to 0.21875
Outputs:
- grad_prev: bfloat16 [2, 2048, 2048], P('section', 'expert')
- grad_gate: bfloat16 [2, 2048, 8], P('section', 'expert')
- grad_w_gate: bfloat16 [2, 16, 2048, 768], P('section', 'expert')
- grad_w_up: bfloat16 [2, 16, 2048, 768], P('section', 'expert')
- grad_w_down: bfloat16 [2, 16, 768, 2048], P('section', 'expert')
The draws below stay inside these ranges and needn't reach their ends.
Inputs may be any that keep to these rules, and one draw needn't show every extreme that they name: `expert_ids`: each token names 8 different experts. In each layer the 128 tokens of one device (aligned blocks of 128 rows) name one expert at most 80 times, and in every draw some device names some expert exactly 80 times.
All inputs are finite; a program needn't handle non-finite values.
Results may differ from the reference program's by a relative error of at most 0.008.
Values may be sent and summed in bfloat16 or wider, within the bound.
A program may use at most 192 MiB of HBM per device.

```python
import math
import jax
import jax.numpy as jnp
import numpy as np
from jax import lax

D = 2048
H = 768
TOPK = 8
TOK_DEV = 128
EXPERTS = 16
LAYERS = 2
TOKENS = 2048
MOST = 80
N_EXPERT = 16


def levels(key, extent, pieces, smallest, high):
    loudness = 1.0
    for dim, blocks in pieces:
        steps = jax.random.uniform(jax.random.fold_in(jax.random.fold_in(key, 6), dim), (blocks,), jnp.float32, smallest / len(pieces), high / len(pieces))
        loudness = loudness * jnp.repeat(jnp.exp(steps), extent[dim] // blocks).reshape((-1,) + (1,) * (len(extent) - 1 - dim))
    return loudness


def deal_out(stream_key, own, number, rows, count, top, limit, skew):
    ranking = jax.random.permutation(stream_key, count)
    heavy_load, usual = shares(count, rows * top, limit, skew, True), shares(count, rows * top, limit, skew, False)
    places = jnp.arange(count)

    def named(lengths, rotation):
        used = int((lengths > 0).sum())
        fixed = max(1, used // 4)
        shifted = fixed + (places - fixed + rotation * (used - fixed)) % max(1, count - fixed)
        return jnp.zeros((count,), jnp.int32).at[ranking[jnp.where(places < fixed, places, shifted)]].set(jnp.asarray(lengths, jnp.int32))

    lengths = jnp.where(number % 4 == 0, named(heavy_load, number // 4), named(usual, number - number // 4 - 1))
    mixed = jax.random.permutation(jax.random.fold_in(own, 3), count)
    giver, taker = mixed[0:count // 2 * 2:2], mixed[1:count // 2 * 2:2]
    room = jnp.minimum(lengths[giver] - 1, limit - lengths[taker]) // 2
    room = jnp.where((giver == ranking[0]) | (taker == ranking[0]) | (lengths[taker] == 0), 0, jnp.maximum(room, 0))
    shifted = jax.random.randint(jax.random.fold_in(own, 4), (count // 2,), 0, 1 << 20) % (room + 1)
    lengths = lengths.at[giver].add(-shifted).at[taker].add(shifted)
    members = jnp.searchsorted(jnp.cumsum(lengths), jnp.arange(rows * top), side="right").astype(jnp.int32)
    listing = members.reshape(top, rows).T
    listing = listing[jax.random.permutation(jax.random.fold_in(own, 1), rows)]
    rotation = jax.random.randint(jax.random.fold_in(own, 2), (rows, 1), 0, top)
    return jnp.take_along_axis(listing, (jnp.arange(top)[None, :] + rotation) % top, axis=1)


def shares(number_of, total, bound, lean, full):
    weights = [(1 << 20) // math.isqrt(rank ** lean) + 1 for rank in range(1, number_of + 1)]
    largest = bound if full else min(bound, max(-(-total // number_of), total * weights[0] // sum(weights)))
    least = 1 if total - largest >= number_of - 1 else 0
    holding, spare = [largest] + [least] * (number_of - 1), total - largest - least * (number_of - 1)
    while spare > 0:
        movable = [i for i in range(1, number_of) if holding[i] < largest] or [i for i in range(1, number_of) if holding[i] < bound]
        mass, budget = sum([weights[i] for i in movable]), spare
        for i in movable:
            addition = min(bound - holding[i], max(1, budget * weights[i] // mass), spare)
            holding[i] = holding[i] + addition
            spare = spare - addition
    return np.array(holding)


def normal_values(key, shape, spread, reach, split=(), held_as=jnp.bfloat16):
    result = spread * jax.random.normal(key, shape, jnp.float32)
    if split:
        result = result * levels(key, shape, split, -0.22, 0.18)
    return jnp.clip(result, -reach, reach).astype(held_as)


def setup_inputs(seed: int = 0) -> dict:
    seeds = jax.random.split(jax.random.key(seed), 8)
    hidden = normal_values(seeds[0], (LAYERS, TOKENS, D), 1.0, 6.0, ((0, 2), (1, 16)))
    out_grad = normal_values(seeds[1], (LAYERS, TOKENS, D), 1.0, 6.0, ((0, 2), (1, 16)))
    expert_ids_keys = jax.random.split(jax.random.fold_in(seeds[2], 1), LAYERS * TOKENS // TOK_DEV)
    expert_ids_turns = jax.random.permutation(jax.random.fold_in(seeds[2], 3), LAYERS * TOKENS // TOK_DEV)
    expert_ids = jax.vmap(lambda own, number: deal_out(jax.random.fold_in(seeds[2], 2), own, number, TOK_DEV, EXPERTS, TOPK, MOST, 2))(expert_ids_keys, expert_ids_turns).reshape((LAYERS, TOKENS, TOPK))
    gate_weight = jnp.clip(jnp.exp(math.log(0.5) - 2.816508 * jax.random.uniform(seeds[3], (LAYERS, TOKENS, TOPK), jnp.float32) ** levels(seeds[3], (LAYERS, TOKENS, TOPK), ((0, 2), (1, 16)), -0.2, 0.2)), 0.029907227, 0.5).astype(jnp.bfloat16)
    w_gate = normal_values(seeds[4], (LAYERS, EXPERTS, D, H), D ** -0.5, 0.125, ((0, 2), (1, 16)))
    w_up = normal_values(seeds[5], (LAYERS, EXPERTS, D, H), D ** -0.5, 0.125, ((0, 2), (1, 16)))
    w_down = normal_values(seeds[6], (LAYERS, EXPERTS, H, D), H ** -0.5, 0.21875, ((0, 2), (1, 16)))
    return dict(hidden=hidden, out_grad=out_grad, expert_ids=expert_ids, gate_weight=gate_weight, w_gate=w_gate, w_up=w_up, w_down=w_down)


def expert_rows(x_rows, dy_rows, g_rows, w_gate_e, w_up_e, w_down_e):
    pre_gate = jnp.dot(x_rows, w_gate_e, preferred_element_type=jnp.float32)
    pre_up = jnp.dot(x_rows, w_up_e, preferred_element_type=jnp.float32)
    sigma = jax.nn.sigmoid(pre_gate)
    active = pre_gate * sigma
    hidden_rows = (active * pre_up).astype(jnp.bfloat16)
    outputs = jnp.dot(hidden_rows, w_down_e, preferred_element_type=jnp.float32)
    gate_grad = jnp.sum(dy_rows.astype(jnp.float32) * outputs, axis=1).astype(jnp.bfloat16)
    backward = jnp.dot(dy_rows, w_down_e.T, preferred_element_type=jnp.float32)
    scale = g_rows.astype(jnp.float32)[:, None]
    scaled_dy = (scale * dy_rows.astype(jnp.float32)).astype(jnp.bfloat16)
    grad_hidden = scale * backward
    grad_a = (grad_hidden * pre_up * sigma * (1.0 + pre_gate * (1.0 - sigma))).astype(jnp.bfloat16)
    grad_b = (grad_hidden * active).astype(jnp.bfloat16)
    row_grad = (jnp.dot(grad_a, w_gate_e.T, preferred_element_type=jnp.float32)
                + jnp.dot(grad_b, w_up_e.T, preferred_element_type=jnp.float32)).astype(jnp.bfloat16)
    sum_gate = jnp.dot(x_rows.T, grad_a, preferred_element_type=jnp.float32)
    sum_up = jnp.dot(x_rows.T, grad_b, preferred_element_type=jnp.float32)
    sum_down = jnp.dot(hidden_rows.T, scaled_dy, preferred_element_type=jnp.float32)
    return row_grad, gate_grad, sum_gate, sum_up, sum_down


def layer_grads(inputs):
    x, dy, ids, gates, w_gate_l, w_up_l, w_down_l = inputs
    tokens, topk = ids.shape
    experts = w_gate_l.shape[0]
    width = x.shape[1]
    capacity = N_EXPERT * MOST
    routes = tokens * topk
    flat = ids.reshape(-1).astype(jnp.int32)
    hits = (flat[:, None] == jnp.arange(experts, dtype=jnp.int32)[None, :]).astype(jnp.int32)
    rank = jnp.sum((jnp.cumsum(hits, axis=0) - 1) * hits, axis=1).astype(jnp.int32)
    route_ids = jnp.arange(routes, dtype=jnp.int32)
    table = jnp.full((experts, capacity), routes, jnp.int32).at[flat, rank].set(route_ids)
    x_pad = jnp.concatenate([x, jnp.zeros((1, width), x.dtype)], axis=0)
    dy_pad = jnp.concatenate([dy, jnp.zeros((1, width), dy.dtype)], axis=0)
    g_pad = jnp.concatenate([gates.reshape(-1), jnp.zeros((1,), gates.dtype)], axis=0)

    def one_expert(args):
        slots, w_gate_e, w_up_e, w_down_e = args
        owner = (slots // topk).astype(jnp.int32)
        return expert_rows(x_pad[owner], dy_pad[owner], g_pad[slots], w_gate_e, w_up_e, w_down_e)

    row_grad, gate_grad, sum_gate, sum_up, sum_down = lax.map(one_expert, (table, w_gate_l, w_up_l, w_down_l))
    flat_slots = table.reshape(-1)
    gathered = jnp.zeros((routes + 1, width), jnp.float32).at[flat_slots].add(row_grad.reshape(-1, width).astype(jnp.float32))
    grad_in = jnp.sum(gathered[:routes].reshape(tokens, topk, width), axis=1).astype(jnp.bfloat16)
    grad_gate = jnp.zeros((routes + 1,), jnp.bfloat16).at[flat_slots].set(gate_grad.reshape(-1))[:routes].reshape(tokens, topk)
    return grad_in, grad_gate, sum_gate.astype(jnp.bfloat16), sum_up.astype(jnp.bfloat16), sum_down.astype(jnp.bfloat16)


def reference(hidden, out_grad, expert_ids, gate_weight, w_gate, w_up, w_down):
    grad_in, grad_gate, grad_w_gate, grad_w_up, grad_w_down = lax.map(
        layer_grads, (hidden, out_grad, expert_ids, gate_weight, w_gate, w_up, w_down))
    grad_prev = jnp.concatenate([grad_in[1:], jnp.zeros_like(grad_in[:1])], axis=0)
    return grad_prev, grad_gate, grad_w_gate, grad_w_up, grad_w_down
```

```python
import functools

import jax
import jax.numpy as jnp
from jax import lax
from jax.experimental import pallas as pl
from jax.experimental.pallas import tpu as pltpu
from jax.sharding import PartitionSpec as P

MESH = pl.DeviceIdType.MESH
SLOT = 80
BF = jnp.bfloat16
F32 = jnp.float32
NT = (((1,), (1,)), ((), ()))
TN = (((0,), (0,)), ((), ()))


def plane_at(k, z):
    half = z // 2
    zz = z + half * (3 - 2 * z)
    hk = k // 2
    p0 = (1 - hk) * ((k + zz) % 2) + hk * k
    return p0 + half * (3 - 2 * p0)


def kernel(
    x_in, dy_in, ids_t, g_t, wg_in, wu_in, wd_in,
    gin_out, gg_out, dwg_out, dwu_out, dwd_out,
    G, META, Xc, Yc, Dx, Hc, Ac, Bc, wg, wu, wd, GG, RF, RD, RZ, RFg, RDg, RZg, SG, SU, SD,
    load_sem, in_sem, out_sem, in_meta, out_meta,
    rs_in, rs_out, rz_in, rz_out, st_sem,
):
    tok, width = x_in.shape
    units = wg.shape[1]
    sec = lax.axis_index("section")
    me = lax.axis_index("expert")
    z, y, x = me // 4, (me // 2) % 2, me % 2
    cx = y * 2 + (1 - x)
    cy = (1 - y) * 2 + x
    cd = (1 - y) * 2 + (1 - x)
    co = y * 2 + x
    to_x = (sec, z * 4 + cx)
    to_y = (sec, z * 4 + cy)
    to_up = (sec, me + 4)
    to_dn = (sec, me - 4)
    has_up = z < 3
    has_dn = z > 0

    loads = []
    for n, (src, dst) in enumerate(
        ((x_in, G.at[0, me]), (dy_in, G.at[1, me]), (wg_in, wg), (wu_in, wu), (wd_in, wd))
    ):
        c = pltpu.make_async_copy(src, dst, load_sem.at[n])
        c.start()
        loads.append(c)

    experts = lax.broadcasted_iota(jnp.int32, (16, tok), 0)
    hit = jnp.zeros((16, tok), F32)
    gsum = jnp.zeros((16, tok), F32)
    for k in range(ids_t.shape[0]):
        same = (ids_t[k : k + 1, :] == experts).astype(F32)
        hit = hit + same
        gsum = gsum + same * g_t[k : k + 1, :]
    before = (
        lax.broadcasted_iota(jnp.int32, (tok, tok), 0) < lax.broadcasted_iota(jnp.int32, (tok, tok), 1)
    ).astype(BF)
    rank = jnp.dot(hit.astype(BF), before, preferred_element_type=F32)
    rank = jnp.where(hit > 0, rank, -1.0)
    META[me, 0:16, :] = rank.astype(BF)
    META[me, 16:32, :] = gsum.astype(BF)

    barrier = pltpu.get_barrier_semaphore()
    pl.semaphore_signal(barrier, inc=1, device_id=to_x, device_id_type=MESH)
    pl.semaphore_signal(barrier, inc=1, device_id=to_y, device_id_type=MESH)

    @pl.when(has_up)
    def _():
        pl.semaphore_signal(barrier, inc=1, device_id=to_up, device_id_type=MESH)

    @pl.when(has_dn)
    def _():
        pl.semaphore_signal(barrier, inc=1, device_id=to_dn, device_id_type=MESH)

    pl.semaphore_wait(barrier, 2 + (5 - z) // 3 + (z + 2) // 3)

    def block_copy(arr, blk, way, to):
        if arr == 2:
            return pltpu.make_async_remote_copy(
                META.at[blk], META.at[blk], out_meta.at[blk, way], in_meta.at[blk],
                device_id=to, device_id_type=MESH)
        return pltpu.make_async_remote_copy(
            G.at[arr, blk], G.at[arr, blk], out_sem.at[arr, blk, way], in_sem.at[arr, blk],
            device_id=to, device_id_type=MESH)

    def arrive(arr, blk):
        block_copy(arr, blk, 0, to_x).wait_recv()

    loads[0].wait()
    loads[1].wait()

    for arr in (2, 0, 1):
        @pl.when(has_up)
        def _(arr=arr):
            block_copy(arr, me, 2, to_up).start()

        @pl.when(has_dn)
        def _(arr=arr):
            block_copy(arr, me, 3, to_dn).start()

        block_copy(arr, me, 0, to_x).start()
        block_copy(arr, me, 1, to_y).start()
    for c in loads[2:]:
        c.wait()

    def own_step(k):
        p = plane_at(k, z)
        blk = p * 4 + co
        for arr in (2, 0, 1):
            arrive(arr, blk)

            @pl.when((p > z) & has_dn)
            def _(arr=arr):
                block_copy(arr, blk, 3, to_dn).start()

            @pl.when((p < z) & has_up)
            def _(arr=arr):
                block_copy(arr, blk, 2, to_up).start()

            block_copy(arr, blk, 0, to_x).start()
            block_copy(arr, blk, 1, to_y).start()

    def side_step(k):
        p = plane_at(k, z)
        for arr in (2, 0, 1):
            arrive(arr, p * 4 + cx)
            if arr != 1:
                block_copy(arr, p * 4 + cx, 1, to_y).start()
            arrive(arr, p * 4 + cy)
            if arr == 1:
                block_copy(arr, p * 4 + cy, 0, to_x).start()

    expert_row = lax.broadcasted_iota(jnp.int32, (16, tok), 0) == me

    def onehot(blk):
        r = jnp.sum(jnp.where(expert_row, META[blk, 0:16, :].astype(F32), 0.0), axis=0, keepdims=True)
        slots = lax.broadcasted_iota(jnp.int32, (SLOT, tok), 0).astype(F32)
        return (slots == r).astype(F32)

    def group(k):
        p = plane_at(k, z)
        for arr in (2, 0, 1):
            arrive(arr, p * 4 + cd)
        base = k * (4 * SLOT)
        rows = pl.ds(pl.multiple_of(base, 4 * SLOT), 4 * SLOT)
        scales, picks = [], []
        for i, c in enumerate((co, cx, cy, cd)):
            blk = p * 4 + c
            pick = onehot(blk)
            gs = jnp.sum(jnp.where(expert_row, META[blk, 16:32, :].astype(F32), 0.0), axis=0, keepdims=True)
            scales.append(jnp.sum(pick * gs, axis=1, keepdims=True))
            picks.append(pick)
            part = pl.ds(pl.multiple_of(base + i * SLOT, SLOT), SLOT)
            pb = pick.astype(BF)

            def gather(j, _, pb=pb, blk=blk, part=part):
                cols = pl.ds(pl.multiple_of(j * 512, 512), 512)
                Xc[part, cols] = jnp.dot(pb, G[0, blk, :, cols], preferred_element_type=F32).astype(BF)
                Yc[part, cols] = jnp.dot(pb, G[1, blk, :, cols], preferred_element_type=F32).astype(BF)
                return 0

            lax.fori_loop(0, width // 512, gather, 0)
        scale = jnp.concatenate(scales, axis=0)

        def hidden_chunk(j, total):
            cols = pl.ds(pl.multiple_of(j * 256, 256), 256)
            a = jnp.dot(Xc[rows, :], wg[:, cols], preferred_element_type=F32)
            b = jnp.dot(Xc[rows, :], wu[:, cols], preferred_element_type=F32)
            back = lax.dot_general(Yc[rows, :], wd[cols, :], NT, preferred_element_type=F32)
            s = jax.nn.sigmoid(a)
            active = a * s
            h = (active * b).astype(BF)
            Hc[rows, cols] = h
            dh = scale * back
            Ac[rows, cols] = (dh * b * s * (1.0 + a * (1.0 - s))).astype(BF)
            Bc[rows, cols] = (dh * active).astype(BF)
            return total + jnp.sum(h.astype(F32) * back, axis=1, keepdims=True)

        total = lax.fori_loop(0, units // 256, hidden_chunk, jnp.zeros((4 * SLOT, 1), F32))
        for i, c in enumerate((co, cx, cy, cd)):
            row = jnp.sum(picks[i] * total[i * SLOT : (i + 1) * SLOT], axis=0, keepdims=True)
            GG[p * 4 + c] = jnp.where(expert_row, row, 0.0).astype(BF)

        def input_chunk(j, _):
            cols = pl.ds(pl.multiple_of(j * 256, 256), 256)
            Yc[rows, cols] = (scale * Yc[rows, cols].astype(F32)).astype(BF)
            d = lax.dot_general(Ac[rows, :], wg[cols, :], NT, preferred_element_type=F32)
            d = d + lax.dot_general(Bc[rows, :], wu[cols, :], NT, preferred_element_type=F32)
            Dx[rows, cols] = d.astype(BF)
            return 0

        lax.fori_loop(0, width // 256, input_chunk, 0)

    def ag_step(k, _):
        @pl.when(k < 3)
        def _():
            own_step(k + 1)

        @pl.when(k < 4)
        def _():
            side_step(k)

        @pl.when(k > 0)
        def _():
            group(k - 1)

        return 0

    lax.fori_loop(0, 5, ag_step, 0)

    def drain(k, _):
        p = plane_at(k, z)
        blk = p * 4 + co
        for arr in (0, 1, 2):
            block_copy(arr, blk, 0, to_x).wait_send()
            block_copy(arr, blk, 1, to_y).wait_send()

            @pl.when(has_up & (p <= z))
            def _(arr=arr):
                block_copy(arr, blk, 2, to_up).wait_send()

            @pl.when(has_dn & (p >= z))
            def _(arr=arr):
                block_copy(arr, blk, 3, to_dn).wait_send()

            if arr != 1:
                block_copy(arr, p * 4 + cx, 1, to_y).wait_send()
            else:
                block_copy(arr, p * 4 + cy, 0, to_x).wait_send()
        return 0

    lax.fori_loop(0, 4, drain, 0)

    halves = tok // 2
    TOP, LOW = pl.ds(0, halves), pl.ds(halves, halves)

    def back_copy(n, k):
        p = plane_at(k, z)
        src, dst, to = (
            (G.at[0, p * 4 + cd, TOP, :], RD.at[0, k], to_x),
            (G.at[0, p * 4 + cd, LOW, :], RD.at[1, k], to_y),
            (GG.at[p * 4 + cd], RDg.at[k], to_x),
            (G.at[0, p * 4 + cx], RF.at[0, k], to_x),
            (G.at[0, p * 4 + cy], RF.at[1, k], to_y),
            (GG.at[p * 4 + cx], RFg.at[0, k], to_x),
            (GG.at[p * 4 + cy], RFg.at[1, k], to_y),
        )[n]
        return pltpu.make_async_remote_copy(
            src, dst, rs_out.at[n, k], rs_in.at[n, k], device_id=to, device_id_type=MESH)

    def line_copy(n, t, down):
        blk = t * 4 + co
        d = 1 if down else 0
        src, dst = ((G.at[0, blk], RZ.at[d, t]), (GG.at[blk], RZg.at[d, t]))[n]
        return pltpu.make_async_remote_copy(
            src, dst, rz_out.at[n, t], rz_in.at[n, d, t],
            device_id=to_dn if down else to_up, device_id_type=MESH)

    def spread(i, _):
        k = 3 - i
        p = plane_at(k, z)
        for n, c in ((3, cd), (1, cx), (2, cy), (0, co)):
            blk = p * 4 + c
            pb = onehot(blk).astype(BF)
            part = pl.ds(pl.multiple_of(k * (4 * SLOT) + n * SLOT, SLOT), SLOT)

            def put(j, _, pb=pb, blk=blk, part=part):
                cols = pl.ds(pl.multiple_of(j * 512, 512), 512)
                G[0, blk, :, cols] = lax.dot_general(
                    pb, Dx[part, cols], TN, preferred_element_type=F32).astype(BF)
                return 0

            lax.fori_loop(0, width // 512, put, 0)
            if n == 3:
                for m in (0, 1, 2):
                    back_copy(m, k).start()
        return 0

    lax.fori_loop(0, 4, spread, 0)

    def second(k):
        p = plane_at(k, z)
        for n in (0, 1, 2):
            back_copy(n, k).wait_recv()
        by, bx = p * 4 + cy, p * 4 + cx
        G[0, by, TOP, :] = (G[0, by, TOP, :].astype(F32) + RD[0, k].astype(F32)).astype(BF)
        GG[by] = (GG[by].astype(F32) + RDg[k].astype(F32)).astype(BF)
        G[0, bx, LOW, :] = (G[0, bx, LOW, :].astype(F32) + RD[1, k].astype(F32)).astype(BF)
        for n in (3, 4, 5, 6):
            back_copy(n, k).start()

    def stores(c, buf):
        cols = pl.ds(pl.multiple_of(c * 256, 256), 256)
        return (
            pltpu.make_async_copy(SG.at[buf], dwg_out.at[cols, :], st_sem.at[0, buf]),
            pltpu.make_async_copy(SU.at[buf], dwu_out.at[cols, :], st_sem.at[1, buf]),
            pltpu.make_async_copy(SD.at[buf], dwd_out.at[:, cols], st_sem.at[2, buf]),
        )

    def weights(c):
        buf = c % 2
        cols = pl.ds(pl.multiple_of(c * 256, 256), 256)

        @pl.when(c >= 2)
        def _():
            for s in stores(c - 2, buf):
                s.wait()

        xt = Xc[:, cols]
        SG[buf] = lax.dot_general(xt, Ac[...], TN, preferred_element_type=F32).astype(BF)
        SU[buf] = lax.dot_general(xt, Bc[...], TN, preferred_element_type=F32).astype(BF)
        SD[buf] = lax.dot_general(Hc[...], Yc[:, cols], TN, preferred_element_type=F32).astype(BF)
        for s in stores(c, buf):
            s.start()

    def third(k):
        p = plane_at(k, z)
        for n in (3, 4, 5, 6):
            back_copy(n, k).wait_recv()
        blk = p * 4 + co
        s = G[0, blk].astype(F32) + RF[0, k].astype(F32) + RF[1, k].astype(F32)
        sg = GG[blk].astype(F32) + RFg[0, k].astype(F32) + RFg[1, k].astype(F32)
        G[0, blk] = s.astype(BF)
        GG[blk] = sg.astype(BF)

        @pl.when(has_up & (p <= z))
        def _():
            line_copy(0, p, True).wait_recv()
            line_copy(1, p, True).wait_recv()
            G[0, blk] = (G[0, blk].astype(F32) + RZ[1, p].astype(F32)).astype(BF)
            GG[blk] = (GG[blk].astype(F32) + RZg[1, p].astype(F32)).astype(BF)

        @pl.when(has_dn & (p >= z))
        def _():
            line_copy(0, p, False).wait_recv()
            line_copy(1, p, False).wait_recv()
            G[0, blk] = (G[0, blk].astype(F32) + RZ[0, p].astype(F32)).astype(BF)
            GG[blk] = (GG[blk].astype(F32) + RZg[0, p].astype(F32)).astype(BF)

        @pl.when(p < z)
        def _():
            line_copy(0, p, True).start()
            line_copy(1, p, True).start()

        @pl.when(p > z)
        def _():
            line_copy(0, p, False).start()
            line_copy(1, p, False).start()

    def rs_step(i, _):
        @pl.when(i < 4)
        def _():
            second(3 - i)
            weights(2 * i)
            weights(2 * i + 1)

        @pl.when(i > 0)
        def _():
            third(4 - i)

        return 0

    lax.fori_loop(0, 5, rs_step, 0)
    gin_out[...] = G[0, me]
    gg_out[...] = GG[me]

    def finish(k, _):
        p = plane_at(k, z)
        for n in range(7):
            back_copy(n, k).wait_send()

        @pl.when(p < z)
        def _():
            line_copy(0, p, True).wait_send()
            line_copy(1, p, True).wait_send()

        @pl.when(p > z)
        def _():
            line_copy(0, p, False).wait_send()
            line_copy(1, p, False).wait_send()

        return 0

    lax.fori_loop(0, 4, finish, 0)
    for c in (6, 7):
        for s in stores(c, c % 2):
            s.wait()


def layer(x, dy, ids_t, g_t, wg, wu, wd):
    tok, width = x.shape
    units = wg.shape[1]
    n = lax.axis_size("expert")
    rows = n * SLOT
    dma = pltpu.SemaphoreType.DMA
    return pl.pallas_call(
        kernel,
        out_shape=(
            jax.ShapeDtypeStruct((tok, width), BF),
            jax.ShapeDtypeStruct((n, tok), BF),
            jax.ShapeDtypeStruct((width, units), BF),
            jax.ShapeDtypeStruct((width, units), BF),
            jax.ShapeDtypeStruct((units, width), BF),
        ),
        in_specs=[pl.BlockSpec(memory_space=pl.ANY)] * 2
        + [pl.BlockSpec(memory_space=pltpu.VMEM)] * 2
        + [pl.BlockSpec(memory_space=pl.ANY)] * 3,
        out_specs=(pl.BlockSpec(memory_space=pltpu.VMEM),) * 2
        + (pl.BlockSpec(memory_space=pl.ANY),) * 3,
        scratch_shapes=[
            pltpu.VMEM((2, n, tok, width), BF),
            pltpu.VMEM((n, 32, tok), BF),
            pltpu.VMEM((rows, width), BF),
            pltpu.VMEM((rows, width), BF),
            pltpu.VMEM((rows, width), BF),
            pltpu.VMEM((rows, units), BF),
            pltpu.VMEM((rows, units), BF),
            pltpu.VMEM((rows, units), BF),
            pltpu.VMEM((width, units), BF),
            pltpu.VMEM((width, units), BF),
            pltpu.VMEM((units, width), BF),
            pltpu.VMEM((n, 16, tok), BF),
            pltpu.VMEM((2, 4, tok, width), BF),
            pltpu.VMEM((2, 4, tok // 2, width), BF),
            pltpu.VMEM((2, 4, tok, width), BF),
            pltpu.VMEM((2, 4, 16, tok), BF),
            pltpu.VMEM((4, 16, tok), BF),
            pltpu.VMEM((2, 4, 16, tok), BF),
            pltpu.VMEM((2, 256, units), BF),
            pltpu.VMEM((2, 256, units), BF),
            pltpu.VMEM((2, units, 256), BF),
            dma((5,)),
            dma((2, n)),
            dma((2, n, 4)),
            dma((n,)),
            dma((n, 4)),
            dma((7, 4)),
            dma((7, 4)),
            dma((2, 2, 4)),
            dma((2, 4)),
            dma((3, 2)),
        ],
        compiler_params=pltpu.CompilerParams(
            collective_id=0, has_side_effects=True, vmem_limit_bytes=64 * 1024 * 1024 - 65536
        ),
        cost_estimate=pl.CostEstimate(flops=33_000_000_000, bytes_accessed=22_000_000, transcendentals=1_000_000),
    )(x, dy, ids_t, g_t, wg, wu, wd)


def on_device(hidden, out_grad, expert_ids, gate_weight, w_gate, w_up, w_down):
    ids_t = expert_ids[0].T
    g_t = gate_weight[0].T.astype(F32)
    grad_in, table, dwg, dwu, dwd = layer(
        hidden[0], out_grad[0], ids_t, g_t, w_gate[0, 0], w_up[0, 0], w_down[0, 0])
    experts = jnp.arange(table.shape[0], dtype=jnp.int32)
    own = ids_t[:, None, :] == experts[None, :, None]
    grad_gate = jnp.sum(jnp.where(own, table[None].astype(F32), 0.0), axis=1).T.astype(BF)
    sections = range(lax.axis_size("section"))
    grad_prev = lax.ppermute(grad_in, "section", [(i + 1, i) for i in sections if i + 1 in sections])
    return grad_prev[None], grad_gate[None], dwg[None, None], dwu[None, None], dwd[None, None]


def solution(mesh):
    wide = P("section", "expert", None)
    deep = P("section", "expert", None, None)
    return jax.shard_map(
        on_device,
        mesh=mesh,
        in_specs=(wide, wide, wide, wide, deep, deep, deep),
        out_specs=(wide, wide, deep, deep, deep),
        check_vma=False,
    )
```

```python
import functools

import jax
import jax.numpy as jnp
from jax import lax
from jax.experimental import pallas as pl
from jax.experimental.pallas import tpu as pltpu
from jax.sharding import PartitionSpec as P

MESH = pl.DeviceIdType.MESH
SLOT = 80
BF = jnp.bfloat16
F32 = jnp.float32
NT = (((1,), (1,)), ((), ()))
TN = (((0,), (0,)), ((), ()))


def plane_at(k, z):
    half = z // 2
    zz = z + half * (3 - 2 * z)
    hk = k // 2
    p0 = (1 - hk) * ((k + zz) % 2) + hk * k
    return p0 + half * (3 - 2 * p0)


def kernel(
    x_in, dy_in, ids_t, g_t, wg_in, wu_in, wd_in,
    gin_out, gg_out, dwg_out, dwu_out, dwd_out,
    G, META, Xc, Yc, Dx, Hc, Ac, Bc, wg, wu, wd, GG, SX, RL, BK, RB, RZ, RFg, RGg, RZg, SG, SU, SD,
    load_sem, in_sem, out_sem, in_meta, out_meta,
    side_in, side_out, rs_in, rs_out, rz_in, rz_out, st_sem,
):
    tok, width = x_in.shape
    units = wg.shape[1]
    sec = lax.axis_index("section")
    me = lax.axis_index("expert")
    z, y, x = me // 4, (me // 2) % 2, me % 2
    cx = y * 2 + (1 - x)
    cy = (1 - y) * 2 + x
    cd = (1 - y) * 2 + (1 - x)
    co = y * 2 + x
    to_x = (sec, z * 4 + cx)
    to_y = (sec, z * 4 + cy)
    to_up = (sec, me + 4)
    to_dn = (sec, me - 4)
    has_up = z < 3
    has_dn = z > 0

    loads = []
    for n, (src, dst) in enumerate(
        ((x_in, G.at[0, z]), (dy_in, G.at[1, z]), (wg_in, wg), (wu_in, wu), (wd_in, wd))
    ):
        c = pltpu.make_async_copy(src, dst, load_sem.at[n])
        c.start()
        loads.append(c)

    experts = lax.broadcasted_iota(jnp.int32, (16, tok), 0)
    hit = jnp.zeros((16, tok), F32)
    gsum = jnp.zeros((16, tok), F32)
    for k in range(ids_t.shape[0]):
        same = (ids_t[k : k + 1, :] == experts).astype(F32)
        hit = hit + same
        gsum = gsum + same * g_t[k : k + 1, :]
    before = (
        lax.broadcasted_iota(jnp.int32, (tok, tok), 0) < lax.broadcasted_iota(jnp.int32, (tok, tok), 1)
    ).astype(BF)
    rank = jnp.dot(hit.astype(BF), before, preferred_element_type=F32)
    rank = jnp.where(hit > 0, rank, -1.0)
    META[me, 0:16, :] = rank.astype(BF)
    META[me, 16:32, :] = gsum.astype(BF)

    barrier = pltpu.get_barrier_semaphore()
    pl.semaphore_signal(barrier, inc=1, device_id=to_x, device_id_type=MESH)
    pl.semaphore_signal(barrier, inc=1, device_id=to_y, device_id_type=MESH)

    @pl.when(has_up)
    def _():
        pl.semaphore_signal(barrier, inc=1, device_id=to_up, device_id_type=MESH)

    @pl.when(has_dn)
    def _():
        pl.semaphore_signal(barrier, inc=1, device_id=to_dn, device_id_type=MESH)

    pl.semaphore_wait(barrier, 2 + (5 - z) // 3 + (z + 2) // 3)

    def line(arr, p, way, to):
        return pltpu.make_async_remote_copy(
            G.at[arr, p], G.at[arr, p], out_sem.at[arr, p, way], in_sem.at[arr, p],
            device_id=to, device_id_type=MESH)

    def meta(blk, way, to):
        return pltpu.make_async_remote_copy(
            META.at[blk], META.at[blk], out_meta.at[blk, way], in_meta.at[blk],
            device_id=to, device_id_type=MESH)

    def part(k, i):
        return pl.ds(pl.multiple_of(k * (4 * SLOT) + i * SLOT, SLOT), SLOT)

    def side(n, k):
        src, dst, to = (
            (SX.at[0, 0, k], Xc.at[part(k, 1), :], to_x),
            (SX.at[1, 0, k], Yc.at[part(k, 1), :], to_x),
            (SX.at[0, 1, k], Xc.at[part(k, 2), :], to_y),
            (SX.at[1, 1, k], Yc.at[part(k, 2), :], to_y),
            (SX.at[0, 2, k], RL.at[0, k], to_x),
            (SX.at[1, 2, k], RL.at[1, k], to_y),
            (RL.at[0, k], Xc.at[part(k, 3), :], to_y),
            (RL.at[1, k], Yc.at[part(k, 3), :], to_x),
        )[n]
        return pltpu.make_async_remote_copy(
            src, dst, side_out.at[n, k], side_in.at[n, k], device_id=to, device_id_type=MESH)

    expert_row = lax.broadcasted_iota(jnp.int32, (16, tok), 0)

    def table_row(blk, first, expert):
        rows = META[blk, first : first + 16, :].astype(F32)
        return jnp.sum(jnp.where(expert_row == expert, rows, 0.0), axis=0, keepdims=True)

    def onehot(blk, expert):
        slots = lax.broadcasted_iota(jnp.int32, (SLOT, tok), 0).astype(F32)
        return (slots == table_row(blk, 0, expert)).astype(F32)

    def compact(k):
        p = plane_at(k, z)
        for i, c in ((3, cd), (1, cx), (2, cy), (0, co)):
            pb = onehot(p * 4 + co, z * 4 + c).astype(BF)

            def pack(j, _, pb=pb, i=i):
                cols = pl.ds(pl.multiple_of(j * 512, 512), 512)
                px = jnp.dot(pb, G[0, p, :, cols], preferred_element_type=F32).astype(BF)
                py = jnp.dot(pb, G[1, p, :, cols], preferred_element_type=F32).astype(BF)
                if i == 0:
                    Xc[part(k, 0), cols] = px
                    Yc[part(k, 0), cols] = py
                else:
                    SX[0, i - 1, k, :, cols] = px
                    SX[1, i - 1, k, :, cols] = py
                return 0

            lax.fori_loop(0, width // 512, pack, 0)
            for n in ((), (0, 1), (2, 3), (4, 5))[i]:
                side(n, k).start()

    loads[0].wait()
    loads[1].wait()

    @pl.when(has_up)
    def _():
        meta(me, 2, to_up).start()
        line(0, z, 0, to_up).start()
        line(1, z, 0, to_up).start()

    @pl.when(has_dn)
    def _():
        meta(me, 3, to_dn).start()
        line(0, z, 1, to_dn).start()
        line(1, z, 1, to_dn).start()

    meta(me, 0, to_x).start()
    meta(me, 1, to_y).start()
    compact(0)
    for c in loads[2:]:
        c.wait()

    def own_step(k):
        p = plane_at(k, z)
        blk = p * 4 + co
        meta(blk, 0, to_x).wait_recv()

        @pl.when((p > z) & has_dn)
        def _():
            meta(blk, 3, to_dn).start()

        @pl.when((p < z) & has_up)
        def _():
            meta(blk, 2, to_up).start()

        meta(blk, 0, to_x).start()
        meta(blk, 1, to_y).start()
        for arr in (0, 1):
            line(arr, p, 0, to_up).wait_recv()

            @pl.when((p > z) & has_dn)
            def _(arr=arr):
                line(arr, p, 1, to_dn).start()

            @pl.when((p < z) & has_up)
            def _(arr=arr):
                line(arr, p, 0, to_up).start()

        compact(k)

    def side_step(k):
        p = plane_at(k, z)
        meta(p * 4 + cx, 0, to_x).wait_recv()
        meta(p * 4 + cx, 1, to_y).start()
        side(4, k).wait_recv()
        side(6, k).start()
        side(5, k).wait_recv()
        side(7, k).start()
        meta(p * 4 + cy, 0, to_x).wait_recv()

    LEFT, RIGHT = pl.ds(0, width // 2), pl.ds(width // 2, width // 2)

    def back_copy(n, k):
        p = plane_at(k, z)
        slot = [pl.ds(i * SLOT, SLOT) for i in range(3)]
        src, dst, to = (
            (Dx.at[part(k, 1), :], BK.at[k, slot[0], :], to_x),
            (Dx.at[part(k, 2), :], BK.at[k, slot[1], :], to_y),
            (Dx.at[part(k, 3), LEFT], RB.at[0, k], to_x),
            (Dx.at[part(k, 3), RIGHT], RB.at[1, k], to_y),
            (RB.at[0, k], BK.at[k, slot[2], LEFT], to_y),
            (RB.at[1, k], BK.at[k, slot[2], RIGHT], to_x),
            (GG.at[p * 4 + cx], RFg.at[0, k], to_x),
            (GG.at[p * 4 + cy], RFg.at[1, k], to_y),
            (GG.at[p * 4 + cd], RGg.at[k], to_x),
            (RGg.at[k], RFg.at[2, k], to_y),
        )[n]
        return pltpu.make_async_remote_copy(
            src, dst, rs_out.at[n, k], rs_in.at[n, k], device_id=to, device_id_type=MESH)

    def send_back(k):
        for n in (2, 3, 8, 6, 7, 0, 1):
            back_copy(n, k).start()

    def group(k):
        p = plane_at(k, z)
        meta(p * 4 + cd, 0, to_x).wait_recv()
        for n in (0, 1, 2, 3, 6, 7):
            side(n, k).wait_recv()

        @pl.when(k == 3)
        def _():
            send_back(0)

        rows = pl.ds(pl.multiple_of(k * (4 * SLOT), 4 * SLOT), 4 * SLOT)
        scales, picks = [], []
        for c in (co, cx, cy, cd):
            pick = onehot(p * 4 + c, me)
            scales.append(jnp.sum(pick * table_row(p * 4 + c, 16, me), axis=1, keepdims=True))
            picks.append(pick)
        scale = jnp.concatenate(scales, axis=0)

        def hidden_chunk(j, total):
            cols = pl.ds(pl.multiple_of(j * 256, 256), 256)
            a = jnp.dot(Xc[rows, :], wg[:, cols], preferred_element_type=F32)
            b = jnp.dot(Xc[rows, :], wu[:, cols], preferred_element_type=F32)
            back = lax.dot_general(Yc[rows, :], wd[cols, :], NT, preferred_element_type=F32)
            s = jax.nn.sigmoid(a)
            active = a * s
            h = (active * b).astype(BF)
            Hc[rows, cols] = h
            dh = scale * back
            Ac[rows, cols] = (dh * b * s * (1.0 + a * (1.0 - s))).astype(BF)
            Bc[rows, cols] = (dh * active).astype(BF)
            return total + jnp.sum(h.astype(F32) * back, axis=1, keepdims=True)

        total = lax.fori_loop(0, units // 256, hidden_chunk, jnp.zeros((4 * SLOT, 1), F32))
        for i, c in enumerate((co, cx, cy, cd)):
            row = jnp.sum(picks[i] * total[i * SLOT : (i + 1) * SLOT], axis=0, keepdims=True)
            GG[p * 4 + c] = jnp.where(expert_row == me, row, 0.0).astype(BF)

        def input_chunk(j, _):
            cols = pl.ds(pl.multiple_of(j * 256, 256), 256)
            Yc[rows, cols] = (scale * Yc[rows, cols].astype(F32)).astype(BF)
            d = lax.dot_general(Ac[rows, :], wg[cols, :], NT, preferred_element_type=F32)
            d = d + lax.dot_general(Bc[rows, :], wu[cols, :], NT, preferred_element_type=F32)
            Dx[rows, cols] = d.astype(BF)
            return 0

        lax.fori_loop(0, width // 256, input_chunk, 0)

    def ag_step(k, _):
        @pl.when(k < 3)
        def _():
            own_step(k + 1)

        @pl.when(k < 4)
        def _():
            side_step(k)

        @pl.when(k > 0)
        def _():
            group(k - 1)

        return 0

    lax.fori_loop(0, 5, ag_step, 0)

    for k in (3, 2, 1):
        send_back(k)

    def drain(k, _):
        p = plane_at(k, z)
        blk = p * 4 + co
        meta(blk, 0, to_x).wait_send()
        meta(blk, 1, to_y).wait_send()
        meta(p * 4 + cx, 1, to_y).wait_send()
        for n in range(8):
            side(n, k).wait_send()

        @pl.when(has_up & (p <= z))
        def _():
            meta(blk, 2, to_up).wait_send()
            for arr in (0, 1):
                line(arr, p, 0, to_up).wait_send()

        @pl.when(has_dn & (p >= z))
        def _():
            meta(blk, 3, to_dn).wait_send()
            for arr in (0, 1):
                line(arr, p, 1, to_dn).wait_send()

        return 0

    lax.fori_loop(0, 4, drain, 0)

    def line_copy(n, t, down):
        blk = t * 4 + co
        d = 1 if down else 0
        src, dst = ((G.at[0, t], RZ.at[d, t]), (GG.at[blk], RZg.at[d, t]))[n]
        return pltpu.make_async_remote_copy(
            src, dst, rz_out.at[n, t], rz_in.at[n, d, t],
            device_id=to_dn if down else to_up, device_id_type=MESH)

    def second(k):
        back_copy(2, k).wait_recv()
        back_copy(4, k).start()
        back_copy(3, k).wait_recv()
        back_copy(5, k).start()
        back_copy(8, k).wait_recv()
        back_copy(9, k).start()

    def stores(c, buf):
        cols = pl.ds(pl.multiple_of(c * 256, 256), 256)
        return (
            pltpu.make_async_copy(SG.at[buf], dwg_out.at[cols, :], st_sem.at[0, buf]),
            pltpu.make_async_copy(SU.at[buf], dwu_out.at[cols, :], st_sem.at[1, buf]),
            pltpu.make_async_copy(SD.at[buf], dwd_out.at[:, cols], st_sem.at[2, buf]),
        )

    def weights(c):
        buf = c % 2
        cols = pl.ds(pl.multiple_of(c * 256, 256), 256)

        @pl.when(c >= 2)
        def _():
            for s in stores(c - 2, buf):
                s.wait()

        xt = Xc[:, cols]
        SG[buf] = lax.dot_general(xt, Ac[...], TN, preferred_element_type=F32).astype(BF)
        SU[buf] = lax.dot_general(xt, Bc[...], TN, preferred_element_type=F32).astype(BF)
        SD[buf] = lax.dot_general(Hc[...], Yc[:, cols], TN, preferred_element_type=F32).astype(BF)
        for s in stores(c, buf):
            s.start()

    def third(k):
        p = plane_at(k, z)
        for n in (0, 1, 4, 5, 6, 7, 9):
            back_copy(n, k).wait_recv()
        blk = p * 4 + co
        first = onehot(blk, me).astype(BF)
        rest = jnp.concatenate([onehot(blk, z * 4 + c) for c in (cx, cy, cd)], axis=0).astype(BF)

        def spread(j, _):
            cols = pl.ds(pl.multiple_of(j * 512, 512), 512)
            total = lax.dot_general(first, Dx[part(k, 0), cols], TN, preferred_element_type=F32)
            total = total + lax.dot_general(rest, BK[k, :, cols], TN, preferred_element_type=F32)
            G[0, p, :, cols] = total.astype(BF)
            return 0

        lax.fori_loop(0, width // 512, spread, 0)
        sg = GG[blk].astype(F32)
        for n in range(3):
            sg = sg + RFg[n, k].astype(F32)
        GG[blk] = sg.astype(BF)

        @pl.when(has_up & (p <= z))
        def _():
            line_copy(0, p, True).wait_recv()
            line_copy(1, p, True).wait_recv()
            G[0, p] = (G[0, p].astype(F32) + RZ[1, p].astype(F32)).astype(BF)
            GG[blk] = (GG[blk].astype(F32) + RZg[1, p].astype(F32)).astype(BF)

        @pl.when(has_dn & (p >= z))
        def _():
            line_copy(0, p, False).wait_recv()
            line_copy(1, p, False).wait_recv()
            G[0, p] = (G[0, p].astype(F32) + RZ[0, p].astype(F32)).astype(BF)
            GG[blk] = (GG[blk].astype(F32) + RZg[0, p].astype(F32)).astype(BF)

        @pl.when(p < z)
        def _():
            line_copy(0, p, True).start()
            line_copy(1, p, True).start()

        @pl.when(p > z)
        def _():
            line_copy(0, p, False).start()
            line_copy(1, p, False).start()

    def rs_step(i, _):
        @pl.when(i < 4)
        def _():
            second(3 - i)
            weights(2 * i)
            weights(2 * i + 1)

        @pl.when(i > 0)
        def _():
            third(4 - i)

        return 0

    lax.fori_loop(0, 5, rs_step, 0)
    gin_out[...] = G[0, z]
    gg_out[...] = GG[me]

    def finish(k, _):
        p = plane_at(k, z)
        for n in range(10):
            back_copy(n, k).wait_send()

        @pl.when(p < z)
        def _():
            line_copy(0, p, True).wait_send()
            line_copy(1, p, True).wait_send()

        @pl.when(p > z)
        def _():
            line_copy(0, p, False).wait_send()
            line_copy(1, p, False).wait_send()

        return 0

    lax.fori_loop(0, 4, finish, 0)
    for c in (6, 7):
        for s in stores(c, c % 2):
            s.wait()


def layer(x, dy, ids_t, g_t, wg, wu, wd):
    tok, width = x.shape
    units = wg.shape[1]
    n = lax.axis_size("expert")
    rows = n * SLOT
    dma = pltpu.SemaphoreType.DMA
    return pl.pallas_call(
        kernel,
        out_shape=(
            jax.ShapeDtypeStruct((tok, width), BF),
            jax.ShapeDtypeStruct((n, tok), BF),
            jax.ShapeDtypeStruct((width, units), BF),
            jax.ShapeDtypeStruct((width, units), BF),
            jax.ShapeDtypeStruct((units, width), BF),
        ),
        in_specs=[pl.BlockSpec(memory_space=pl.ANY)] * 2
        + [pl.BlockSpec(memory_space=pltpu.VMEM)] * 2
        + [pl.BlockSpec(memory_space=pl.ANY)] * 3,
        out_specs=(pl.BlockSpec(memory_space=pltpu.VMEM),) * 2
        + (pl.BlockSpec(memory_space=pl.ANY),) * 3,
        scratch_shapes=[
            pltpu.VMEM((2, 4, tok, width), BF),
            pltpu.VMEM((n, 32, tok), BF),
            pltpu.VMEM((rows, width), BF),
            pltpu.VMEM((rows, width), BF),
            pltpu.VMEM((rows, width), BF),
            pltpu.VMEM((rows, units), BF),
            pltpu.VMEM((rows, units), BF),
            pltpu.VMEM((rows, units), BF),
            pltpu.VMEM((width, units), BF),
            pltpu.VMEM((width, units), BF),
            pltpu.VMEM((units, width), BF),
            pltpu.VMEM((n, 16, tok), BF),
            pltpu.VMEM((2, 3, 4, SLOT, width), BF),
            pltpu.VMEM((2, 4, SLOT, width), BF),
            pltpu.VMEM((4, 3 * SLOT, width), BF),
            pltpu.VMEM((2, 4, SLOT, width // 2), BF),
            pltpu.VMEM((2, 4, tok, width), BF),
            pltpu.VMEM((3, 4, 16, tok), BF),
            pltpu.VMEM((4, 16, tok), BF),
            pltpu.VMEM((2, 4, 16, tok), BF),
            pltpu.VMEM((2, 256, units), BF),
            pltpu.VMEM((2, 256, units), BF),
            pltpu.VMEM((2, units, 256), BF),
            dma((5,)),
            dma((2, 4)),
            dma((2, 4, 2)),
            dma((n,)),
            dma((n, 4)),
            dma((8, 4)),
            dma((8, 4)),
            dma((10, 4)),
            dma((10, 4)),
            dma((2, 2, 4)),
            dma((2, 4)),
            dma((3, 2)),
        ],
        compiler_params=pltpu.CompilerParams(
            collective_id=0, has_side_effects=True, vmem_limit_bytes=64 * 1024 * 1024 - 65536
        ),
        cost_estimate=pl.CostEstimate(flops=33_000_000_000, bytes_accessed=22_000_000, transcendentals=1_000_000),
    )(x, dy, ids_t, g_t, wg, wu, wd)


def on_device(hidden, out_grad, expert_ids, gate_weight, w_gate, w_up, w_down):
    ids_t = expert_ids[0].T
    g_t = gate_weight[0].T.astype(F32)
    grad_in, table, dwg, dwu, dwd = layer(
        hidden[0], out_grad[0], ids_t, g_t, w_gate[0, 0], w_up[0, 0], w_down[0, 0])
    experts = jnp.arange(table.shape[0], dtype=jnp.int32)
    own = ids_t[:, None, :] == experts[None, :, None]
    grad_gate = jnp.sum(jnp.where(own, table[None].astype(F32), 0.0), axis=1).T.astype(BF)
    sections = range(lax.axis_size("section"))
    grad_prev = lax.ppermute(grad_in, "section", [(i + 1, i) for i in sections if i + 1 in sections])
    return grad_prev[None], grad_gate[None], dwg[None, None], dwu[None, None], dwd[None, None]


def solution(mesh):
    wide = P("section", "expert", None)
    deep = P("section", "expert", None, None)
    return jax.shard_map(
        on_device,
        mesh=mesh,
        in_specs=(wide, wide, wide, wide, deep, deep, deep),
        out_specs=(wide, wide, deep, deep, deep),
        check_vma=False,
    )
```
